128 devices in a mesh: dp: 16 (over z_lo, y, core), ctx: 8 (over x, z_hi).
Axes of the slice: x: 4, y: 4, z: 4 (z_hi: 2, z_lo: 2; z = z_hi * 2 + z_lo), core: 2. Of those that a mesh axis runs over, the one named last changes fastest.
Arguments:
- queries: bfloat16 [16, 8, 384, 4096], P(None, 'ctx', 'dp'), may hold values from -200 to 200
- keys: bfloat16 [16, 8, 384, 512], P(None, 'ctx', 'dp'), may hold values from -6 to 6
- values: bfloat16 [16, 8, 384, 512], P(None, 'ctx', 'dp'), may hold values from -6 to 6
- doc_lengths: int32 [64], replicated, may hold values from 1 to 1152, 49152 in all
Outputs:
- attended: bfloat16 [16, 8, 384, 4096], P(None, 'ctx', 'dp')
The draws below stay inside these ranges and needn't reach their ends.
Inputs may be any that keep to these rules, and one draw needn't show every extreme that they name: `doc_lengths`: the 64 lengths sum to 49152; the longest is exactly 1152.
All inputs are finite; a program needn't handle non-finite values.
Results may differ from the reference program's by a relative error of at most 0.024.
Values may be sent and summed in bfloat16 or wider, within the bound.
No kernel may reach another device: no remote copies, remote signals or barrier semaphores. Data moves between devices by JAX's collectives and lax.ppermute only.
A program may use at most 128 MiB of HBM per device.

```python
import math
import jax
import jax.numpy as jnp
import numpy as np
from jax import lax

QUERY_HEADS = 32
KEY_VALUE_HEADS = 4
HEAD_WIDTH = 128
TOKENS_PER_BLOCK = 384
DOCS = 64
LEN = 49152
N_DP = 16
N_CTX = 8


def draw_queries(key, part):
    key = jax.random.fold_in(key, 11)
    shape = (N_DP, N_CTX, TOKENS_PER_BLOCK, QUERY_HEADS * HEAD_WIDTH)
    return jnp.clip(jax.random.normal(key, shape, jnp.float32), -6.0, 6.0).astype(jnp.bfloat16)


def steps_of(rng, dims, split, least, largest):
    loudness, own = 1.0, jax.random.fold_in(rng, 6)
    for position, parts in split:
        steps = jnp.exp(jax.random.uniform(jax.random.fold_in(own, position), (parts,), jnp.float32, least / len(split), largest / len(split)))
        loudness = loudness * jnp.repeat(steps, dims[position] // parts).reshape([-1 if axis == position else 1 for axis in range(len(dims))])
    return loudness


def split_up(amount, total, most, slope):
    loads = [(1 << 20) // math.isqrt(grade ** slope) + 1 for grade in range(2, amount + 1)]
    rest, holding = total - most - (amount - 1), [1] * (amount - 1)
    while rest > 0:
        free = [i for i in range(amount - 1) if holding[i] < most]
        mass, remaining = sum([loads[i] for i in free]), rest
        for i in free:
            extra = min(most - holding[i], max(1, remaining * loads[i] // mass), rest)
            holding[i] = holding[i] + extra
            rest = rest - extra
    return np.array([most] + holding)


def uneven(stream_key, count, total, most, skew):
    if count == 2:
        one = jax.random.randint(stream_key, (), max(1, total - most), min(most, total - 1) + 1)
        return jnp.stack([one, total - one])
    lengths = jnp.asarray(split_up(count, total, most, skew), jnp.int32)
    couples = (count - 1) // 2
    source_of, receiver = lengths[1:1 + 2 * couples:2], lengths[2:2 + 2 * couples:2]
    margin = jnp.minimum(source_of - 1, most - receiver)
    passed = jax.random.randint(jax.random.fold_in(stream_key, 1), (couples,), 0, 1 << 20) % (margin + 1)
    lengths = lengths.at[1:1 + 2 * couples:2].set(source_of - passed).at[2:2 + 2 * couples:2].set(receiver + passed)
    return lengths[jax.random.permutation(jax.random.fold_in(stream_key, 2), count)]


def centred(stream_key, extent, deviation, limit, pieces=(), kind=jnp.bfloat16):
    factor_of = steps_of(stream_key, extent, pieces, -0.22, 0.18) if pieces else 1.0
    drawn = jax.random.normal(stream_key, extent, jnp.float32) * deviation * factor_of
    return jnp.minimum(jnp.maximum(drawn, -limit), limit).astype(kind)


def setup_inputs(seed: int = 0) -> dict:
    key_list = jax.random.split(jax.random.key(seed), 5)
    queries = draw_queries(jax.random.fold_in(key_list[4], 71), 0)
    keys = centred(key_list[1], (N_DP, N_CTX, TOKENS_PER_BLOCK, KEY_VALUE_HEADS * HEAD_WIDTH), 1.0, 6.0, ((1, 8), (2, 16)))
    values = centred(key_list[2], (N_DP, N_CTX, TOKENS_PER_BLOCK, KEY_VALUE_HEADS * HEAD_WIDTH), 1.0, 6.0, ((1, 8), (2, 16)))
    doc_lengths = uneven(key_list[3], DOCS, LEN, 3 * TOKENS_PER_BLOCK, 2).astype(jnp.int32)
    return {"queries": queries, "keys": keys, "values": values, "doc_lengths": doc_lengths}


rope_theta = 1000000.0

def rotary_embedding(field, token_positions):
    half_size = field.shape[-1] // 2
    exponent = jnp.arange(half_size, dtype=jnp.float32) * (2.0 / field.shape[-1])
    frequency = jnp.exp(-exponent * jnp.log(jnp.float32(rope_theta)))
    angles = token_positions.astype(jnp.float32)[:, None] * frequency[None, :]
    cosine = jnp.cos(angles)[:, None, :]
    sine = jnp.sin(angles)[:, None, :]
    first = field[..., :half_size].astype(jnp.float32)
    second = field[..., half_size:].astype(jnp.float32)
    turned = jnp.concatenate([first * cosine - second * sine, second * cosine + first * sine], axis=-1)
    return turned.astype(jnp.bfloat16)

def doc_index(token_positions, doc_ends):
    return lax.optimization_barrier(jnp.sum((token_positions[:, None] >= doc_ends[None, :]).astype(jnp.int32), axis=1))

def attend(query_matrix, key_matrix, value_matrix, allowed):
    count_of_rows = query_matrix.shape[0]
    queries_per_group = QUERY_HEADS // KEY_VALUE_HEADS
    grouped_scores = query_matrix.reshape(count_of_rows, KEY_VALUE_HEADS, queries_per_group, HEAD_WIDTH)
    scale = 1.0 / jnp.sqrt(jnp.float32(HEAD_WIDTH))

    def single_group(index):
        query_part = lax.dynamic_index_in_dim(grouped_scores, index, 1, keepdims=False).astype(jnp.float32)
        key_part = lax.dynamic_index_in_dim(key_matrix, index, 1, keepdims=False).astype(jnp.float32)
        value_part = lax.dynamic_index_in_dim(value_matrix, index, 1, keepdims=False).astype(jnp.float32)
        scores = jnp.einsum('tpd,kd->ptk', query_part, key_part) * scale
        scores = jnp.where(allowed[None], scores, -jnp.inf)
        highest = lax.optimization_barrier(jnp.max(scores, axis=-1, keepdims=True))
        weights = jnp.exp(scores - highest)
        totals = lax.optimization_barrier(jnp.sum(weights, axis=-1, keepdims=True))
        rounded = weights.astype(jnp.bfloat16).astype(jnp.float32)
        return jnp.einsum('ptk,kd->ptd', rounded, value_part) / totals
    stacked_heads = lax.map(single_group, jnp.arange(KEY_VALUE_HEADS, dtype=jnp.int32))
    return jnp.transpose(stacked_heads, (2, 0, 1, 3)).reshape(count_of_rows, QUERY_HEADS * HEAD_WIDTH).astype(jnp.bfloat16)

def reference(queries, keys, values, doc_lengths):
    block_count = N_DP * N_CTX
    sequence_length = block_count * TOKENS_PER_BLOCK
    token_positions = jnp.arange(sequence_length, dtype=jnp.int32)
    query_matrix = rotary_embedding(queries.reshape(sequence_length, QUERY_HEADS, HEAD_WIDTH), token_positions)
    key_matrix = rotary_embedding(keys.reshape(sequence_length, KEY_VALUE_HEADS, HEAD_WIDTH), token_positions)
    value_matrix = values.reshape(sequence_length, KEY_VALUE_HEADS, HEAD_WIDTH)
    padding_amount = jnp.zeros((3 * TOKENS_PER_BLOCK, KEY_VALUE_HEADS, HEAD_WIDTH), jnp.bfloat16)
    key_padded = jnp.concatenate([padding_amount, key_matrix], axis=0)
    value_padded = jnp.concatenate([padding_amount, value_matrix], axis=0)
    doc_ends = jnp.cumsum(doc_lengths, dtype=jnp.int32)

    def one_block(block):
        start = block * TOKENS_PER_BLOCK
        query_block = lax.dynamic_slice_in_dim(query_matrix, start, TOKENS_PER_BLOCK, 0)
        key_block = lax.dynamic_slice_in_dim(key_padded, start, 4 * TOKENS_PER_BLOCK, 0)
        value_block = lax.dynamic_slice_in_dim(value_padded, start, 4 * TOKENS_PER_BLOCK, 0)
        query_positions = start + jnp.arange(TOKENS_PER_BLOCK, dtype=jnp.int32)
        key_positions = start - 3 * TOKENS_PER_BLOCK + jnp.arange(4 * TOKENS_PER_BLOCK, dtype=jnp.int32)
        same_doc = doc_index(query_positions, doc_ends)[:, None] == doc_index(key_positions, doc_ends)[None, :]
        allowed = same_doc & (key_positions[None, :] <= query_positions[:, None]) & (key_positions[None, :] >= 0)
        return attend(query_block, key_block, value_block, allowed)
    result = lax.map(one_block, jnp.arange(block_count, dtype=jnp.int32))
    return result.reshape(N_DP, N_CTX, TOKENS_PER_BLOCK, QUERY_HEADS * HEAD_WIDTH)
```

```python
import jax
import jax.numpy as jnp
from jax import lax
from jax.experimental import pallas as pl
from jax.experimental.pallas import tpu as pltpu
from jax.sharding import Mesh, PartitionSpec as P

QUERY_HEADS = 32
KEY_VALUE_HEADS = 4
HEAD_WIDTH = 128
ROPE_THETA = 1000000.0

PAIR = 768
HALO = 1152
KEYS = HALO + PAIR
HEADS = 16
KV = 2
PER_KV = 8
TILE = 128
WINDOW = 256
STEPS = PAIR // TILE
MOST = (HALO + TILE) // WINDOW
SCALE = 1.4426950408889634 / 128.0**0.5
LOW = -1e30


def rotated(field, cosine, sine):
    wide = field.astype(jnp.float32)
    return (wide * cosine + pltpu.roll(wide, HEAD_WIDTH // 2, 1) * sine).astype(jnp.bfloat16)


def attend_kernel(
    first_ref, q_ref, own_ref, near_ref, far_ref, cos_ref, sin_ref, start_ref, out_ref,
    k_ref, v_ref, bias_ref, qr_ref,
):
    step = pl.program_id(0)

    @pl.when(step == 0)
    def _():
        base = 0
        for ref in (far_ref, near_ref, own_ref):
            rows = ref.shape[0]
            for piece in range(0, rows, TILE):
                here = pl.ds(base + piece, TILE)
                cosine, sine = cos_ref[here, :], sin_ref[here, :]
                for head in range(KV):
                    wide = pl.ds(head * HEAD_WIDTH, HEAD_WIDTH)
                    k_ref[head, here, :] = rotated(ref[pl.ds(piece, TILE), wide], cosine, sine)
                    v_ref[head, here, :HEAD_WIDTH] = ref[
                        pl.ds(piece, TILE), pl.ds((KV + head) * HEAD_WIDTH, HEAD_WIDTH)
                    ]
                    v_ref[head, here, HEAD_WIDTH:] = jnp.ones((TILE, HEAD_WIDTH), jnp.bfloat16)
            base += rows

    here = pl.ds(pl.multiple_of(HALO + step * TILE, TILE), TILE)
    cosine, sine = cos_ref[here, :], sin_ref[here, :]
    for head in range(HEADS):
        qr_ref[head // 2, pl.ds((head % 2) * TILE, TILE), :] = rotated(
            q_ref[:, pl.ds(head * HEAD_WIDTH, HEAD_WIDTH)], cosine, sine
        )
    stop = step * TILE + HALO + TILE
    windows = (stop - first_ref[step] + WINDOW - 1) // WINDOW

    for count in range(1, MOST + 1):

        @pl.when(windows == count)
        def _():
            width = count * WINDOW
            begin = pl.multiple_of(stop - width, TILE)
            span = pl.ds(begin, width)
            place = begin + lax.broadcasted_iota(jnp.int32, (TILE, width), 1)
            row = step * TILE + HALO + lax.broadcasted_iota(jnp.int32, (TILE, width), 0)
            allowed = (place >= start_ref[:, :1]) & (place <= row)
            bias_ref[:, :width] = jnp.where(allowed, 0.0, LOW)

            for group in range(HEADS // 2):
                kv = group // (PER_KV // 2)
                scores = lax.dot_general(
                    qr_ref[group],
                    k_ref[kv, span, :],
                    (((1,), (1,)), ((), ())),
                    preferred_element_type=jnp.float32,
                )
                bias = bias_ref[:, :width]
                scores = (scores.reshape(2, TILE, width) + bias[None]).reshape(2 * TILE, width)
                top = jnp.max(scores, axis=1, keepdims=True)
                weights = jnp.exp2((scores - top) * SCALE).astype(jnp.bfloat16)
                mixed = jnp.dot(weights, v_ref[kv, span, :], preferred_element_type=jnp.float32)
                result = (mixed[:, :HEAD_WIDTH] / mixed[:, HEAD_WIDTH:]).astype(jnp.bfloat16)
                for part in range(2):
                    out_ref[:, pl.ds((2 * group + part) * HEAD_WIDTH, HEAD_WIDTH)] = result[
                        part * TILE : (part + 1) * TILE
                    ]


def attend(first, q, own, near, far, cosine, sine, start):
    whole = lambda shape: pl.BlockSpec(shape, lambda i, f: (0, 0))
    return pl.pallas_call(
        attend_kernel,
        grid_spec=pltpu.PrefetchScalarGridSpec(
            num_scalar_prefetch=1,
            grid=(STEPS,),
            in_specs=[
                pl.BlockSpec((TILE, HEADS * HEAD_WIDTH), lambda i, f: (i, 0)),
                whole((PAIR, 2 * KV * HEAD_WIDTH)),
                whole((PAIR, 2 * KV * HEAD_WIDTH)),
                whole((HALO - PAIR, 2 * KV * HEAD_WIDTH)),
                whole((KEYS, HEAD_WIDTH)),
                whole((KEYS, HEAD_WIDTH)),
                pl.BlockSpec((TILE, 1), lambda i, f: (i, 0)),
            ],
            out_specs=pl.BlockSpec((TILE, HEADS * HEAD_WIDTH), lambda i, f: (i, 0)),
            scratch_shapes=[
                pltpu.VMEM((KV, KEYS, HEAD_WIDTH), jnp.bfloat16),
                pltpu.VMEM((KV, KEYS, 2 * HEAD_WIDTH), jnp.bfloat16),
                pltpu.VMEM((TILE, MOST * WINDOW), jnp.float32),
                pltpu.VMEM((HEADS // 2, 2 * TILE, HEAD_WIDTH), jnp.bfloat16),
            ],
        ),
        out_shape=jax.ShapeDtypeStruct((PAIR, HEADS * HEAD_WIDTH), jnp.bfloat16),
        compiler_params=pltpu.CompilerParams(
            dimension_semantics=("arbitrary",), vmem_limit_bytes=56 * 1024 * 1024
        ),
        cost_estimate=pl.CostEstimate(
            flops=8_000_000_000, bytes_accessed=10_000_000, transcendentals=12_000_000
        ),
        name="attend",
    )(first, q, own, near, far, cosine, sine, start)


def exchange(value):
    return lax.all_to_all(value, ("zh", "dp"), split_axis=0, concat_axis=0, tiled=True)


def halved(value):
    groups, rows, width = value.shape
    return value.reshape(groups, rows, 2, width // 2).transpose(2, 0, 1, 3)


def moved(value, steps):
    count = lax.axis_size("dp") * lax.axis_size("x")
    pairs = [(2 * i + h, 2 * (i + steps) + h) for i in range(count - steps) for h in range(2)]
    return lax.ppermute(value, ("dp", "x", "zh"), pairs)


def on_device(queries, keys, values, doc_lengths):
    groups, _, rows, _ = queries.shape
    k = halved(keys.reshape(groups, rows, -1))
    v = halved(values.reshape(groups, rows, -1))
    own = exchange(jnp.concatenate([k, v], -1).reshape(2 * groups, rows, -1)).reshape(PAIR, -1)
    near = moved(own, 1)
    far = moved(own[PAIR // 2 :], 2)
    q = exchange(halved(queries.reshape(groups, rows, -1)).reshape(2 * groups, rows, -1))

    base = (lax.axis_index("dp") * lax.axis_size("x") + lax.axis_index("x")) * PAIR
    positions = base - HALO + jnp.arange(KEYS, dtype=jnp.int32)
    half = HEAD_WIDTH // 2
    exponent = jnp.arange(half, dtype=jnp.float32) * (2.0 / HEAD_WIDTH)
    frequency = jnp.exp(-exponent * jnp.log(jnp.float32(ROPE_THETA)))
    angles = positions.astype(jnp.float32)[:, None] * frequency[None, :]
    cosine, sine = jnp.cos(angles), jnp.sin(angles)
    cosine = jnp.concatenate([cosine, cosine], -1)
    sine = jnp.concatenate([-sine, sine], -1)

    docs = jnp.arange(doc_lengths.shape[0], dtype=jnp.int32)
    ends = jnp.sum(jnp.where(docs[:, None] <= docs[None, :], doc_lengths[:, None], 0), axis=0)
    mine = positions[HALO:]
    starts = jnp.max(jnp.where(ends[None, :] <= mine[:, None], ends[None, :], 0), axis=1)
    starts = starts - (base - HALO)

    mixed = attend(
        starts[::TILE], q.reshape(PAIR, -1), own, near, far, cosine, sine, starts[:, None]
    )
    back = exchange(mixed.reshape(2 * groups, rows, -1))
    back = back.reshape(2, groups, rows, -1).transpose(1, 2, 0, 3)
    return back.reshape(queries.shape)


def solution(mesh):
    fine = Mesh(mesh.devices.reshape(16, 4, 2), ("dp", "x", "zh"))
    spec = P(None, ("x", "zh"), "dp", None)
    return jax.shard_map(
        on_device, mesh=fine, in_specs=(spec, spec, spec, P()), out_specs=spec, check_vma=False
    )
```

```python
import jax
import jax.numpy as jnp
from jax import lax
from jax.experimental import pallas as pl
from jax.experimental.pallas import tpu as pltpu
from jax.sharding import Mesh, PartitionSpec as P

QUERY_HEADS = 32
KEY_VALUE_HEADS = 4
WIDTH = 128
HALF = WIDTH // 2
ROPE_THETA = 1000000.0
GROUPS = 16
ROWS = 24
GROUP = 3072
PAIR = 768
HALO = 1152
FAR = HALO - PAIR
SLOTS = 2
PER_KV = QUERY_HEADS // KEY_VALUE_HEADS
PEERS = 32
PIECE = PER_KV * ROWS
TILE = 96
SOURCES = TILE // ROWS
WINDOW = 256
STEPS = PAIR // TILE
MOST = 5
REACH = MOST * WINDOW
PAD = REACH - HALO - TILE
KEYS = PAD + HALO + PAIR
PARTS = 2
SCALE = 1.4426950408889634 / WIDTH**0.5
LOW = -1e30
MIB = 1024 * 1024

HBM = pl.BlockSpec(memory_space=pltpu.HBM)
VMEM = pl.BlockSpec(memory_space=pltpu.VMEM)
SMEM = pl.BlockSpec(memory_space=pltpu.SMEM)


def resident(value):
    return pltpu.with_memory_space_constraint(value, pltpu.VMEM)


def stored(value):
    return pltpu.with_memory_space_constraint(value, pltpu.HBM)


def small(limit, **rest):
    return dict(compiler_params=pltpu.CompilerParams(vmem_limit_bytes=limit * MIB), **rest)


def rotated(field, cosine, sine):
    wide = field.astype(jnp.float32)
    return wide * cosine + pltpu.roll(wide, HALF, wide.ndim - 1) * sine


def split_keys_kernel(k_ref, v_ref, out_ref, held, sems, out_sems):
    arrivals = []
    for head in range(KEY_VALUE_HEADS):
        for index, ref in enumerate((k_ref, v_ref)):
            arrivals.append(
                pltpu.make_async_copy(
                    ref.at[:, :, pl.ds(head * WIDTH, WIDTH)],
                    held.at[head, :, index],
                    sems.at[head * 2 + index],
                )
            )
    for copy in arrivals:
        copy.start()
    leaves = []
    for head in range(KEY_VALUE_HEADS):
        for copy in arrivals[2 * head : 2 * head + 2]:
            copy.wait()
        leaves.append(pltpu.make_async_copy(held.at[head], out_ref.at[head], out_sems.at[head]))
        leaves[-1].start()
    for copy in leaves:
        copy.wait()


def split_keys(keys, values):
    shape = (KEY_VALUE_HEADS, GROUPS, 2, ROWS, WIDTH)
    return pl.pallas_call(
        split_keys_kernel,
        in_specs=[HBM, HBM],
        out_specs=HBM,
        out_shape=pltpu.HBM(shape, jnp.bfloat16),
        scratch_shapes=[
            pltpu.VMEM(shape, jnp.bfloat16),
            pltpu.SemaphoreType.DMA((2 * KEY_VALUE_HEADS,)),
            pltpu.SemaphoreType.DMA((KEY_VALUE_HEADS,)),
        ],
        **small(8, name="split_keys"),
    )(stored(keys), stored(values))


def split_queries_kernel(q_ref, cos_ref, sin_ref, out_ref, held, made, sems, out_sems):
    chunk = 4
    arrivals, leaves = [], []
    for part in range(GROUPS // chunk):
        here = pl.ds(part * chunk, chunk)
        arrivals.append(pltpu.make_async_copy(q_ref.at[here], held.at[here], sems.at[part]))
        leaves.append(
            pltpu.make_async_copy(made.at[:, here], out_ref.at[:, here], out_sems.at[part])
        )
    for copy in arrivals:
        copy.start()
    for part in range(GROUPS // chunk):
        arrivals[part].wait()

        def one_group(index, _):
            group = part * chunk + index
            cosine, sine = cos_ref[group], sin_ref[group]
            for head in range(QUERY_HEADS):
                turned = rotated(held[group, :, pl.ds(head * WIDTH, WIDTH)], cosine, sine)
                made[head // PER_KV, group, head % PER_KV] = turned.astype(jnp.bfloat16)
            return 0

        lax.fori_loop(0, chunk, one_group, 0)
        leaves[part].start()
    for copy in leaves:
        copy.wait()


def split_queries(queries, cosine, sine):
    shape = (KEY_VALUE_HEADS, GROUPS, PER_KV, ROWS, WIDTH)
    return pl.pallas_call(
        split_queries_kernel,
        in_specs=[HBM, VMEM, VMEM],
        out_specs=HBM,
        out_shape=pltpu.HBM(shape, jnp.bfloat16),
        scratch_shapes=[
            pltpu.VMEM((GROUPS, ROWS, QUERY_HEADS * WIDTH), jnp.bfloat16),
            pltpu.VMEM(shape, jnp.bfloat16),
            pltpu.SemaphoreType.DMA((4,)),
            pltpu.SemaphoreType.DMA((4,)),
        ],
        cost_estimate=pl.CostEstimate(
            flops=10_000_000, bytes_accessed=6_500_000, transcendentals=0
        ),
        **small(16, name="split_queries"),
    )(stored(queries), resident(cosine), resident(sine))


def join_heads_kernel(in_ref, out_ref, held, sems):
    chunk = 4
    copies = []
    for part in range(GROUPS // chunk):

        def one_group(index, _):
            group = part * chunk + index
            for head in range(QUERY_HEADS):
                held[group, :, pl.ds(head * WIDTH, WIDTH)] = in_ref[
                    head // PER_KV, group, head % PER_KV
                ]
            return 0

        lax.fori_loop(0, chunk, one_group, 0)
        here = pl.ds(part * chunk, chunk)
        copies.append(pltpu.make_async_copy(held.at[here], out_ref.at[here], sems.at[part]))
        copies[-1].start()
    for copy in copies:
        copy.wait()


def join_heads(parts):
    return pl.pallas_call(
        join_heads_kernel,
        in_specs=[VMEM],
        out_specs=HBM,
        out_shape=pltpu.HBM((GROUPS, ROWS, QUERY_HEADS * WIDTH), jnp.bfloat16),
        scratch_shapes=[
            pltpu.VMEM((GROUPS, ROWS, QUERY_HEADS * WIDTH), jnp.bfloat16),
            pltpu.SemaphoreType.DMA((4,)),
        ],
        **small(16, name="join_heads"),
    )(resident(parts))


def turn_keys_kernel(in_ref, cos_ref, sin_ref, *out_refs):
    for slot in range(SLOTS):
        own_ref, far_ref = out_refs[slot], out_refs[SLOTS + slot]
        keys = in_ref[:, slot, 0].astype(jnp.float32).reshape(PAIR, WIDTH)
        values = in_ref[:, slot, 1].astype(jnp.float32).reshape(PAIR, WIDTH)
        keys = rotated(keys, cos_ref[slot], sin_ref[slot]).astype(jnp.bfloat16)
        values = values.astype(jnp.bfloat16)
        own_ref[:, :WIDTH] = keys
        own_ref[:, WIDTH:] = values
        far_ref[:, :WIDTH] = keys[PAIR - FAR :]
        far_ref[:, WIDTH:] = values[PAIR - FAR :]


def turn_keys(own, cosine, sine):
    return pl.pallas_call(
        turn_keys_kernel,
        in_specs=[VMEM] * 3,
        out_specs=[VMEM] * 4,
        out_shape=[jax.ShapeDtypeStruct((PAIR, 2 * WIDTH), jnp.bfloat16)] * 2
        + [jax.ShapeDtypeStruct((FAR, 2 * WIDTH), jnp.bfloat16)] * 2,
        **small(12, name="turn_keys"),
    )(stored(own), cosine, sine)


def attend_kernel(
    first_ref, base_ref, flag_ref, ends_ref, q_ref, own0, own1, near0, near1, far0, far1, out_ref,
    q_held, k_ref, v_ref, start_ref, bias_ref, s_ref, p_ref, q_sems, k_sems, v_sems,
):
    size = PARTS * PIECE
    pieces = []
    for place, (pair, base, flag) in enumerate((
        ((own0, own1), PAD + HALO, 0),
        ((near0, near1), PAD + FAR, flag_ref[1]),
        ((far0, far1), PAD, flag_ref[0]),
    )):
        for index, ref in enumerate(pair):
            to = (flag + index) % SLOTS
            rows = pl.ds(base, ref.shape[0])
            for column, (held, sems) in enumerate(((k_ref, k_sems), (v_ref, v_sems))):
                pieces.append(
                    pltpu.make_async_copy(
                        ref.at[:, pl.ds(column * WIDTH, WIDTH)],
                        held.at[to, rows, :],
                        sems.at[place * SLOTS + index],
                    )
                )
    for copy in pieces:
        copy.start()

    def arrival(index):
        slot, step = index // STEPS, index % STEPS
        return pltpu.make_async_copy(
            q_ref.at[pl.ds(step * SOURCES, SOURCES), slot], q_held.at[index], q_sems.at[index]
        )

    for index in range(SLOTS * STEPS):
        arrival(index).start()
    for slot in range(SLOTS):
        k_ref[slot, :PAD, :] = jnp.zeros((PAD, WIDTH), jnp.bfloat16)
        v_ref[slot, :PAD, :] = jnp.zeros((PAD, WIDTH), jnp.bfloat16)
    for index in range(SLOTS * STEPS):
        base = base_ref[index // STEPS]
        ends = jnp.broadcast_to(ends_ref[...] - base, (TILE, WIDTH))
        own = PAD + HALO + index % STEPS * TILE
        own = own + lax.broadcasted_iota(jnp.int32, (TILE, WIDTH), 0)
        start = jnp.max(jnp.where(ends <= own, ends, -base), axis=1, keepdims=True)
        start_ref[index] = jnp.broadcast_to(start, (TILE, WIDTH))
    for copy in pieces:
        copy.wait()

    def one_step(index, _):
        slot, step = index // STEPS, index % STEPS
        stop = step * TILE + REACH
        windows = (stop - first_ref[index] + WINDOW - 1) // WINDOW
        arrival(index).wait()

        for count in range(1, MOST + 1):

            @pl.when(windows == count)
            def _():
                width = count * WINDOW
                begin = pl.multiple_of(stop - width, 32)
                lane = lax.broadcasted_iota(jnp.int32, (TILE, WIDTH), 1)
                row = stop - TILE + lax.broadcasted_iota(jnp.int32, (TILE, WIDTH), 0)
                start = start_ref[index]
                for column in range(0, width, WIDTH):
                    key = lane + (begin + column)
                    allowed = (key >= start) & (key <= row)
                    bias_ref[:, pl.ds(column, WIDTH)] = jnp.where(allowed, 0.0, LOW)

                def score(turn):
                    q = q_held[index, pl.ds(turn * PARTS, PARTS)].reshape(size, WIDTH)
                    rows = pl.ds(turn * PARTS * ROWS, PARTS * ROWS)
                    top = None
                    for window in range(count):
                        here = pl.ds(pl.multiple_of(begin + window * WINDOW, 32), WINDOW)
                        scores = lax.dot_general(
                            q,
                            k_ref[slot, here, :],
                            (((1,), (1,)), ((), ())),
                            preferred_element_type=jnp.float32,
                        )
                        bias = bias_ref[rows, pl.ds(window * WINDOW, WINDOW)]
                        scores = scores.reshape(PARTS, PER_KV, ROWS, WINDOW)
                        scores = scores + bias.reshape(PARTS, 1, ROWS, WINDOW)
                        scores = scores.reshape(size, WINDOW)
                        s_ref[turn, :, pl.ds(window * WINDOW, WINDOW)] = scores
                        high = jnp.maximum(scores[:, :WIDTH], scores[:, WIDTH:])
                        top = high if top is None else jnp.maximum(top, high)
                    return jnp.max(top, axis=1, keepdims=True)

                def weigh(turn, top):
                    total = None
                    for window in range(count):
                        here = pl.ds(window * WINDOW, WINDOW)
                        weights = jnp.exp2((s_ref[turn, :, here] - top) * SCALE)
                        p_ref[turn, :, here] = weights.astype(jnp.bfloat16)
                        both = weights[:, :WIDTH] + weights[:, WIDTH:]
                        total = both if total is None else total + both
                    return jnp.sum(total, axis=1, keepdims=True)

                def mix(turn, total):
                    mixed = jnp.dot(
                        p_ref[turn, :, :width],
                        v_ref[slot, pl.ds(begin, width), :],
                        preferred_element_type=jnp.float32,
                    )
                    result = (mixed / total).astype(jnp.bfloat16)
                    for part in range(PARTS):
                        out_ref[step * SOURCES + turn * PARTS + part, slot] = result[
                            part * PIECE : (part + 1) * PIECE
                        ]

                turns = SOURCES // PARTS
                tops = [score(0)]
                for turn in range(turns):
                    if turn + 1 < turns:
                        tops.append(score(turn + 1))
                    mix(turn, weigh(turn, tops[turn]))

        return 0

    lax.fori_loop(0, SLOTS * STEPS, one_step, 0)


def attend(first, base, flags, ends, q, own, near, far):
    size = PARTS * PIECE
    turns = SOURCES // PARTS
    return pl.pallas_call(
        attend_kernel,
        in_specs=[SMEM] * 3 + [VMEM] + [HBM] * 7,
        out_specs=VMEM,
        out_shape=pltpu.VMEM((PEERS, SLOTS, PIECE, WIDTH), jnp.bfloat16),
        scratch_shapes=[
            pltpu.VMEM((SLOTS * STEPS, SOURCES, PIECE, WIDTH), jnp.bfloat16),
            pltpu.VMEM((SLOTS, KEYS, WIDTH), jnp.bfloat16),
            pltpu.VMEM((SLOTS, KEYS, WIDTH), jnp.bfloat16),
            pltpu.VMEM((SLOTS * STEPS, TILE, WIDTH), jnp.int32),
            pltpu.VMEM((TILE, REACH), jnp.float32),
            pltpu.VMEM((turns, size, REACH), jnp.float32),
            pltpu.VMEM((turns, size, REACH), jnp.bfloat16),
            pltpu.SemaphoreType.DMA((SLOTS * STEPS,)),
            pltpu.SemaphoreType.DMA((3 * SLOTS,)),
            pltpu.SemaphoreType.DMA((3 * SLOTS,)),
        ],
        cost_estimate=pl.CostEstimate(
            flops=8_000_000_000, bytes_accessed=10_000_000, transcendentals=12_000_000
        ),
        **small(24, name="attend"),
    )(first, base, flags, ends, *map(stored, (q,) + own + near + far))


def exchange(value):
    return lax.all_to_all(value, ("zh", "dp"), split_axis=0, concat_axis=0, tiled=True)


def moved(value, slot, steps):
    pairs = []
    for dp in range(16):
        for x in range(4):
            to = dp
            if x + steps >= 4 and slot == 1:
                if dp % 8 == 7:
                    continue
                to = dp + 1
            for h in range(2):
                pairs.append((dp * 8 + x * 2 + h, to * 8 + (x + steps) % 4 * 2 + h))
    return lax.ppermute(value, ("dp", "x", "zh"), pairs)


def tables(positions):
    lane = jnp.arange(WIDTH, dtype=jnp.int32)
    exponent = (lane % HALF).astype(jnp.float32) * (2.0 / WIDTH)
    frequency = jnp.exp(-exponent * jnp.log(jnp.float32(ROPE_THETA)))
    angles = positions.astype(jnp.float32)[..., None] * frequency
    return jnp.cos(angles), jnp.sin(angles) * jnp.where(lane < HALF, -1.0, 1.0)


def on_device(queries, keys, values, doc_lengths):
    dp, x, zh = lax.axis_index("dp"), lax.axis_index("x"), lax.axis_index("zh")
    own = split_keys(keys.reshape(GROUPS, ROWS, -1), values.reshape(GROUPS, ROWS, -1))
    own = exchange(own.reshape(PEERS, SLOTS, 2, ROWS, WIDTH))

    home = (
        jnp.arange(GROUPS, dtype=jnp.int32)[:, None] * GROUP
        + (x * 2 + zh) * (PAIR // 2)
        + dp * ROWS
        + jnp.arange(ROWS, dtype=jnp.int32)[None, :]
    )
    q = split_queries(queries.reshape(GROUPS, ROWS, -1), *tables(home))
    q = exchange(q.reshape(PEERS, SLOTS, PER_KV, ROWS, WIDTH))

    base = (dp % 8 * SLOTS + jnp.arange(SLOTS, dtype=jnp.int32)) * GROUP + x * PAIR
    positions = base[:, None] + jnp.arange(PAIR, dtype=jnp.int32)[None, :]
    own0, own1, last0, last1 = turn_keys(own, *tables(positions))
    near = moved(own0, 0, 1), moved(own1, 1, 1)
    far = moved(last0, 0, 2), moved(last1, 1, 2)
    flags = jnp.stack([(x < 2).astype(jnp.int32), (x < 1).astype(jnp.int32)])

    docs = jnp.arange(WIDTH, dtype=jnp.int32)
    lengths = jnp.pad(doc_lengths, (0, WIDTH - doc_lengths.shape[0]))
    ends = jnp.sum(jnp.where(docs[:, None] <= docs[None, :], lengths[:, None], 0), axis=0)
    heads = base[:, None] + jnp.arange(0, PAIR, TILE, dtype=jnp.int32)[None, :]
    first = jnp.max(jnp.where(ends <= heads[..., None], ends, 0), axis=-1)
    base = base - PAD - HALO

    mixed = attend(
        (first - base[:, None]).reshape(-1),
        base,
        flags,
        ends[None, :],
        q.reshape(PEERS, SLOTS, PIECE, WIDTH),
        (own0, own1),
        near,
        far,
    )
    back = exchange(mixed.reshape(PEERS, SLOTS, PER_KV, ROWS, WIDTH))
    back = join_heads(back.reshape(KEY_VALUE_HEADS, GROUPS, PER_KV, ROWS, WIDTH))
    return back.reshape(queries.shape)


def solution(mesh):
    fine = Mesh(mesh.devices.reshape(16, 4, 2), ("dp", "x", "zh"))
    spec = P(None, ("x", "zh"), "dp", None)
    return jax.shard_map(
        on_device, mesh=fine, in_specs=(spec, spec, spec, P()), out_specs=spec, check_vma=False
    )
```

```python
import jax
import jax.numpy as jnp
from jax import lax
from jax.experimental import pallas as pl
from jax.experimental.pallas import tpu as pltpu
from jax.sharding import Mesh, PartitionSpec as P

QUERY_HEADS = 32
KEY_VALUE_HEADS = 4
WIDTH = 128
HALF = WIDTH // 2
ROPE_THETA = 1000000.0
GROUPS = 16
ROWS = 24
GROUP = 3072
PAIR = 768
HALO = 1152
FAR = HALO - PAIR
SLOTS = 2
PER_KV = QUERY_HEADS // KEY_VALUE_HEADS
PEERS = 32
PIECE = PER_KV * ROWS
TILE = 48
SOURCES = TILE // ROWS
WINDOW = 256
STEPS = PAIR // TILE
UNITS = SLOTS * STEPS
TEAM = 4
MOST = 5
REACH = MOST * WINDOW
PAD = REACH - HALO - TILE
KEYS = PAD + HALO + PAIR
SIZE = SOURCES * PIECE
SCALE = 1.4426950408889634 / WIDTH**0.5
LOW = -1e30
MIB = 1024 * 1024

HBM = pl.BlockSpec(memory_space=pltpu.HBM)
VMEM = pl.BlockSpec(memory_space=pltpu.VMEM)
SMEM = pl.BlockSpec(memory_space=pltpu.SMEM)


def resident(value):
    return pltpu.with_memory_space_constraint(value, pltpu.VMEM)


def stored(value):
    return pltpu.with_memory_space_constraint(value, pltpu.HBM)


def small(limit, **rest):
    return dict(compiler_params=pltpu.CompilerParams(vmem_limit_bytes=limit * MIB), **rest)


def rotated(field, cosine, sine):
    wide = field.astype(jnp.float32)
    return wide * cosine + pltpu.roll(wide, HALF, wide.ndim - 1) * sine


def split_keys_kernel(k_ref, v_ref, out_ref, held, sems, out_sems):
    arrivals = []
    for head in range(KEY_VALUE_HEADS):
        for index, ref in enumerate((k_ref, v_ref)):
            arrivals.append(
                pltpu.make_async_copy(
                    ref.at[:, :, pl.ds(head * WIDTH, WIDTH)],
                    held.at[head, :, index],
                    sems.at[head * 2 + index],
                )
            )
    for copy in arrivals:
        copy.start()
    leaves = []
    for head in range(KEY_VALUE_HEADS):
        for copy in arrivals[2 * head : 2 * head + 2]:
            copy.wait()
        leaves.append(pltpu.make_async_copy(held.at[head], out_ref.at[head], out_sems.at[head]))
        leaves[-1].start()
    for copy in leaves:
        copy.wait()


def split_keys(keys, values):
    shape = (KEY_VALUE_HEADS, GROUPS, 2, ROWS, WIDTH)
    return pl.pallas_call(
        split_keys_kernel,
        in_specs=[HBM, HBM],
        out_specs=HBM,
        out_shape=pltpu.HBM(shape, jnp.bfloat16),
        scratch_shapes=[
            pltpu.VMEM(shape, jnp.bfloat16),
            pltpu.SemaphoreType.DMA((2 * KEY_VALUE_HEADS,)),
            pltpu.SemaphoreType.DMA((KEY_VALUE_HEADS,)),
        ],
        **small(8, name="split_keys"),
    )(stored(keys), stored(values))


def split_queries_kernel(q_ref, cos_ref, sin_ref, out_ref, held, made, sems, out_sems):
    chunk = 4
    arrivals, leaves = [], []
    for part in range(GROUPS // chunk):
        here = pl.ds(part * chunk, chunk)
        arrivals.append(pltpu.make_async_copy(q_ref.at[here], held.at[here], sems.at[part]))
        leaves.append(
            pltpu.make_async_copy(made.at[:, here], out_ref.at[:, here], out_sems.at[part])
        )
    for copy in arrivals:
        copy.start()
    for part in range(GROUPS // chunk):
        arrivals[part].wait()

        def one_group(index, _):
            group = part * chunk + index
            cosine, sine = cos_ref[group], sin_ref[group]
            for head in range(QUERY_HEADS):
                turned = rotated(held[group, :, pl.ds(head * WIDTH, WIDTH)], cosine, sine)
                made[head // PER_KV, group, head % PER_KV] = turned.astype(jnp.bfloat16)
            return 0

        lax.fori_loop(0, chunk, one_group, 0)
        leaves[part].start()
    for copy in leaves:
        copy.wait()


def split_queries(queries, cosine, sine):
    shape = (KEY_VALUE_HEADS, GROUPS, PER_KV, ROWS, WIDTH)
    return pl.pallas_call(
        split_queries_kernel,
        in_specs=[HBM, VMEM, VMEM],
        out_specs=HBM,
        out_shape=pltpu.HBM(shape, jnp.bfloat16),
        scratch_shapes=[
            pltpu.VMEM((GROUPS, ROWS, QUERY_HEADS * WIDTH), jnp.bfloat16),
            pltpu.VMEM(shape, jnp.bfloat16),
            pltpu.SemaphoreType.DMA((4,)),
            pltpu.SemaphoreType.DMA((4,)),
        ],
        cost_estimate=pl.CostEstimate(
            flops=10_000_000, bytes_accessed=6_500_000, transcendentals=0
        ),
        **small(16, name="split_queries"),
    )(stored(queries), resident(cosine), resident(sine))


def join_heads_kernel(in_ref, out_ref, held, sems):
    chunk = 4
    copies = []
    for part in range(GROUPS // chunk):

        def one_group(index, _):
            group = part * chunk + index
            for head in range(QUERY_HEADS):
                held[group, :, pl.ds(head * WIDTH, WIDTH)] = in_ref[
                    head // PER_KV, group, head % PER_KV
                ]
            return 0

        lax.fori_loop(0, chunk, one_group, 0)
        here = pl.ds(part * chunk, chunk)
        copies.append(pltpu.make_async_copy(held.at[here], out_ref.at[here], sems.at[part]))
        copies[-1].start()
    for copy in copies:
        copy.wait()


def join_heads(parts):
    return pl.pallas_call(
        join_heads_kernel,
        in_specs=[VMEM],
        out_specs=HBM,
        out_shape=pltpu.HBM((GROUPS, ROWS, QUERY_HEADS * WIDTH), jnp.bfloat16),
        scratch_shapes=[
            pltpu.VMEM((GROUPS, ROWS, QUERY_HEADS * WIDTH), jnp.bfloat16),
            pltpu.SemaphoreType.DMA((4,)),
        ],
        **small(16, name="join_heads"),
    )(resident(parts))


def turn_keys_kernel(in_ref, cos_ref, sin_ref, *out_refs):
    for slot in range(SLOTS):
        own_ref, far_ref = out_refs[slot], out_refs[SLOTS + slot]
        keys = in_ref[:, slot, 0].astype(jnp.float32).reshape(PAIR, WIDTH)
        values = in_ref[:, slot, 1].astype(jnp.float32).reshape(PAIR, WIDTH)
        keys = rotated(keys, cos_ref[slot], sin_ref[slot]).astype(jnp.bfloat16)
        values = values.astype(jnp.bfloat16)
        own_ref[:, :WIDTH] = keys
        own_ref[:, WIDTH:] = values
        far_ref[:, :WIDTH] = keys[PAIR - FAR :]
        far_ref[:, WIDTH:] = values[PAIR - FAR :]


def turn_keys(own, cosine, sine):
    return pl.pallas_call(
        turn_keys_kernel,
        in_specs=[VMEM] * 3,
        out_specs=[VMEM] * 4,
        out_shape=[jax.ShapeDtypeStruct((PAIR, 2 * WIDTH), jnp.bfloat16)] * 2
        + [jax.ShapeDtypeStruct((FAR, 2 * WIDTH), jnp.bfloat16)] * 2,
        **small(12, name="turn_keys"),
    )(own, cosine, sine)


def attend_kernel(
    order_ref, most_ref, base_ref, flag_ref, ends_ref, q_ref, own0, own1, near0, near1, far0, far1,
    out_ref, q_held, k_ref, v_ref, start_ref, bias_ref, s_ref, p_ref, q_sems, k_sems, v_sems,
):
    pieces = []
    for place, (pair, base, flag) in enumerate((
        ((own0, own1), PAD + HALO, 0),
        ((near0, near1), PAD + FAR, flag_ref[1]),
        ((far0, far1), PAD, flag_ref[0]),
    )):
        for index, ref in enumerate(pair):
            to = (flag + index) % SLOTS
            rows = pl.ds(base, ref.shape[0])
            for column, (held, sems) in enumerate(((k_ref, k_sems), (v_ref, v_sems))):
                pieces.append(
                    pltpu.make_async_copy(
                        ref.at[:, pl.ds(column * WIDTH, WIDTH)],
                        held.at[to, rows, :],
                        sems.at[place * SLOTS + index],
                    )
                )
    for copy in pieces:
        copy.start()

    def arrival(index):
        slot, step = index // STEPS, index % STEPS
        return pltpu.make_async_copy(
            q_ref.at[pl.ds(step * SOURCES, SOURCES), slot], q_held.at[index], q_sems.at[index]
        )

    for index in range(UNITS):
        arrival(order_ref[index]).start()
    for slot in range(SLOTS):
        k_ref[slot, :PAD, :] = jnp.zeros((PAD, WIDTH), jnp.bfloat16)
        v_ref[slot, :PAD, :] = jnp.zeros((PAD, WIDTH), jnp.bfloat16)
    for index in range(UNITS):
        base = base_ref[index // STEPS]
        ends = jnp.broadcast_to(ends_ref[...] - base, (TILE, WIDTH))
        own = PAD + HALO + index % STEPS * TILE
        own = own + lax.broadcasted_iota(jnp.int32, (TILE, WIDTH), 0)
        start = jnp.max(jnp.where(ends <= own, ends, -base), axis=1, keepdims=True)
        start_ref[index] = jnp.broadcast_to(start, (TILE, WIDTH))
    for copy in pieces:
        copy.wait()

    def one_team(team, _):
        units = [order_ref[team * TEAM + i] for i in range(TEAM)]
        slots = [unit // STEPS for unit in units]
        steps = [unit % STEPS for unit in units]
        stops = [step * TILE + REACH for step in steps]
        for unit in units:
            arrival(unit).wait()

        for count in range(1, MOST + 1):

            @pl.when(most_ref[team] == count)
            def _():
                width = count * WINDOW
                begins = [pl.multiple_of(stop - width, 16) for stop in stops]

                def score(i):
                    lane = lax.broadcasted_iota(jnp.int32, (TILE, WIDTH), 1) + begins[i]
                    row = stops[i] - TILE + lax.broadcasted_iota(jnp.int32, (TILE, WIDTH), 0)
                    start = start_ref[units[i]]
                    for column in range(0, width, WIDTH):
                        key = lane + column
                        allowed = (key >= start) & (key <= row)
                        bias_ref[i, :, pl.ds(column, WIDTH)] = jnp.where(allowed, 0.0, LOW)
                    q = q_held[units[i]].reshape(SIZE, WIDTH)
                    top = None
                    for window in range(count):
                        here = pl.ds(pl.multiple_of(begins[i] + window * WINDOW, 16), WINDOW)
                        scores = lax.dot_general(
                            q,
                            k_ref[slots[i], here, :],
                            (((1,), (1,)), ((), ())),
                            preferred_element_type=jnp.float32,
                        )
                        bias = bias_ref[i, :, pl.ds(window * WINDOW, WINDOW)]
                        scores = scores.reshape(SOURCES, PER_KV, ROWS, WINDOW)
                        scores = scores + bias.reshape(SOURCES, 1, ROWS, WINDOW)
                        scores = scores.reshape(SIZE, WINDOW)
                        s_ref[i, :, pl.ds(window * WINDOW, WINDOW)] = scores
                        high = jnp.maximum(scores[:, :WIDTH], scores[:, WIDTH:])
                        top = high if top is None else jnp.maximum(top, high)
                    return jnp.max(top, axis=1, keepdims=True)

                def weigh(i, top):
                    total = None
                    for window in range(count):
                        here = pl.ds(window * WINDOW, WINDOW)
                        weights = jnp.exp2((s_ref[i, :, here] - top) * SCALE)
                        p_ref[i, :, here] = weights.astype(jnp.bfloat16)
                        both = weights[:, :WIDTH] + weights[:, WIDTH:]
                        total = both if total is None else total + both
                    return jnp.sum(total, axis=1, keepdims=True)

                def mix(i, total):
                    mixed = jnp.dot(
                        p_ref[i, :, :width],
                        v_ref[slots[i], pl.ds(begins[i], width), :],
                        preferred_element_type=jnp.float32,
                    )
                    result = (mixed / total).astype(jnp.bfloat16)
                    out_ref[pl.ds(steps[i] * SOURCES, SOURCES), slots[i]] = result.reshape(
                        SOURCES, PIECE, WIDTH
                    )

                tops = [score(0)]
                for i in range(TEAM):
                    if i + 1 < TEAM:
                        tops.append(score(i + 1))
                    mix(i, weigh(i, tops[i]))

        return 0

    lax.fori_loop(0, UNITS // TEAM, one_team, 0)


def attend(order, most, base, flags, ends, q, own, near, far):
    return pl.pallas_call(
        attend_kernel,
        in_specs=[SMEM] * 4 + [VMEM] + [HBM] * 7,
        out_specs=VMEM,
        out_shape=pltpu.VMEM((PEERS, SLOTS, PIECE, WIDTH), jnp.bfloat16),
        scratch_shapes=[
            pltpu.VMEM((UNITS, SOURCES, PIECE, WIDTH), jnp.bfloat16),
            pltpu.VMEM((SLOTS, KEYS, WIDTH), jnp.bfloat16),
            pltpu.VMEM((SLOTS, KEYS, WIDTH), jnp.bfloat16),
            pltpu.VMEM((UNITS, TILE, WIDTH), jnp.int32),
            pltpu.VMEM((TEAM, TILE, REACH), jnp.float32),
            pltpu.VMEM((TEAM, SIZE, REACH), jnp.float32),
            pltpu.VMEM((TEAM, SIZE, REACH), jnp.bfloat16),
            pltpu.SemaphoreType.DMA((UNITS,)),
            pltpu.SemaphoreType.DMA((3 * SLOTS,)),
            pltpu.SemaphoreType.DMA((3 * SLOTS,)),
        ],
        cost_estimate=pl.CostEstimate(
            flops=8_000_000_000, bytes_accessed=10_000_000, transcendentals=12_000_000
        ),
        **small(32, name="attend"),
    )(order, most, base, flags, ends, *map(stored, (q,) + own + near + far))


def exchange(value):
    return lax.all_to_all(value, ("zh", "dp"), split_axis=0, concat_axis=0, tiled=True)


def moved(value, slot, steps):
    pairs = []
    for dp in range(16):
        for x in range(4):
            to = dp
            if x + steps >= 4 and slot == 1:
                if dp % 8 == 7:
                    continue
                to = dp + 1
            for h in range(2):
                pairs.append((dp * 8 + x * 2 + h, to * 8 + (x + steps) % 4 * 2 + h))
    return lax.ppermute(value, ("dp", "x", "zh"), pairs)


def tables(positions):
    lane = jnp.arange(WIDTH, dtype=jnp.int32)
    exponent = (lane % HALF).astype(jnp.float32) * (2.0 / WIDTH)
    frequency = jnp.exp(-exponent * jnp.log(jnp.float32(ROPE_THETA)))
    angles = positions.astype(jnp.float32)[..., None] * frequency
    return jnp.cos(angles), jnp.sin(angles) * jnp.where(lane < HALF, -1.0, 1.0)


def on_device(queries, keys, values, doc_lengths):
    dp, x, zh = lax.axis_index("dp"), lax.axis_index("x"), lax.axis_index("zh")
    own = split_keys(keys.reshape(GROUPS, ROWS, -1), values.reshape(GROUPS, ROWS, -1))
    own = exchange(own.reshape(PEERS, SLOTS, 2, ROWS, WIDTH))

    home = (
        jnp.arange(GROUPS, dtype=jnp.int32)[:, None] * GROUP
        + (x * 2 + zh) * (PAIR // 2)
        + dp * ROWS
        + jnp.arange(ROWS, dtype=jnp.int32)[None, :]
    )
    base = (dp % 8 * SLOTS + jnp.arange(SLOTS, dtype=jnp.int32)) * GROUP + x * PAIR
    positions = base[:, None] + jnp.arange(PAIR, dtype=jnp.int32)[None, :]
    turns = lax.optimization_barrier((*tables(home), *tables(positions)))
    q = split_queries(queries.reshape(GROUPS, ROWS, -1), *turns[:2])
    q = exchange(q.reshape(PEERS, SLOTS, PER_KV, ROWS, WIDTH))

    own0, own1, last0, last1 = turn_keys(own, *turns[2:])
    near = moved(own0, 0, 1), moved(own1, 1, 1)
    far = moved(last0, 0, 2), moved(last1, 1, 2)
    flags = jnp.stack([(x < 2).astype(jnp.int32), (x < 1).astype(jnp.int32)])

    docs = jnp.arange(WIDTH, dtype=jnp.int32)
    lengths = jnp.pad(doc_lengths, (0, WIDTH - doc_lengths.shape[0]))
    ends = jnp.sum(jnp.where(docs[:, None] <= docs[None, :], lengths[:, None], 0), axis=0)
    heads = base[:, None] + jnp.arange(0, PAIR, TILE, dtype=jnp.int32)[None, :]
    first = jnp.max(jnp.where(ends <= heads[..., None], ends, 0), axis=-1)
    need = (heads + TILE - first + WINDOW - 1) // WINDOW
    need, unit = need.reshape(-1), jnp.arange(UNITS, dtype=jnp.int32)
    earlier = (need[None, :] > need[:, None]) | (
        (need[None, :] == need[:, None]) & (unit[None, :] < unit[:, None])
    )
    rank = jnp.sum(earlier.astype(jnp.int32), axis=1)
    order = jnp.sum(jnp.where(rank[None, :] == unit[:, None], unit[None, :], 0), axis=1)
    most = jnp.sum(jnp.where(rank[None, :] == unit[::TEAM, None], need[None, :], 0), axis=1)
    base = base - PAD - HALO

    mixed = attend(
        order,
        most,
        base,
        flags,
        ends[None, :],
        q.reshape(PEERS, SLOTS, PIECE, WIDTH),
        (own0, own1),
        near,
        far,
    )
    back = exchange(mixed.reshape(PEERS, SLOTS, PER_KV, ROWS, WIDTH))
    back = join_heads(back.reshape(KEY_VALUE_HEADS, GROUPS, PER_KV, ROWS, WIDTH))
    return back.reshape(queries.shape)


def solution(mesh):
    fine = Mesh(mesh.devices.reshape(16, 4, 2), ("dp", "x", "zh"))
    spec = P(None, ("x", "zh"), "dp", None)
    return jax.shard_map(
        on_device, mesh=fine, in_specs=(spec, spec, spec, P()), out_specs=spec, check_vma=False
    )
```

```python
import jax
import jax.numpy as jnp
from jax import lax
from jax.experimental import pallas as pl
from jax.experimental.pallas import tpu as pltpu
from jax.sharding import Mesh, PartitionSpec as P

QUERY_HEADS = 32
KEY_VALUE_HEADS = 4
WIDTH = 128
HALF = WIDTH // 2
ROPE_THETA = 1000000.0
GROUPS = 16
ROWS = 24
GROUP = 3072
PAIR = 768
HALO = 1152
FAR = HALO - PAIR
SLOTS = 2
PER_KV = QUERY_HEADS // KEY_VALUE_HEADS
PEERS = 32
PIECE = PER_KV * ROWS
TILE = 48
SOURCES = TILE // ROWS
WINDOW = 256
STEPS = PAIR // TILE
UNITS = SLOTS * STEPS
TEAM = 4
MOST = 5
REACH = MOST * WINDOW
PAD = REACH - HALO - TILE
KEYS = PAD + HALO + PAIR
SIZE = SOURCES * PIECE
SCALE = 1.4426950408889634 / WIDTH**0.5
LOW = -1e30
MIB = 1024 * 1024

HBM = pl.BlockSpec(memory_space=pltpu.HBM)
VMEM = pl.BlockSpec(memory_space=pltpu.VMEM)
SMEM = pl.BlockSpec(memory_space=pltpu.SMEM)


def resident(value):
    return pltpu.with_memory_space_constraint(value, pltpu.VMEM)


def stored(value):
    return pltpu.with_memory_space_constraint(value, pltpu.HBM)


def small(limit, **rest):
    return dict(compiler_params=pltpu.CompilerParams(vmem_limit_bytes=limit * MIB), **rest)


def rotated(field, cosine, sine):
    wide = field.astype(jnp.float32)
    return wide * cosine + pltpu.roll(wide, HALF, wide.ndim - 1) * sine


def split_keys_kernel(k_ref, v_ref, out_ref, held, sems, out_sems):
    arrivals = []
    for head in range(KEY_VALUE_HEADS):
        for index, ref in enumerate((k_ref, v_ref)):
            arrivals.append(
                pltpu.make_async_copy(
                    ref.at[:, :, pl.ds(head * WIDTH, WIDTH)],
                    held.at[head, :, index],
                    sems.at[head * 2 + index],
                )
            )
    for copy in arrivals:
        copy.start()
    leaves = []
    for head in range(KEY_VALUE_HEADS):
        for copy in arrivals[2 * head : 2 * head + 2]:
            copy.wait()
        leaves.append(pltpu.make_async_copy(held.at[head], out_ref.at[head], out_sems.at[head]))
        leaves[-1].start()
    for copy in leaves:
        copy.wait()


def split_keys(keys, values):
    shape = (KEY_VALUE_HEADS, GROUPS, 2, ROWS, WIDTH)
    return pl.pallas_call(
        split_keys_kernel,
        in_specs=[HBM, HBM],
        out_specs=HBM,
        out_shape=pltpu.HBM(shape, jnp.bfloat16),
        scratch_shapes=[
            pltpu.VMEM(shape, jnp.bfloat16),
            pltpu.SemaphoreType.DMA((2 * KEY_VALUE_HEADS,)),
            pltpu.SemaphoreType.DMA((KEY_VALUE_HEADS,)),
        ],
        **small(8, name="split_keys"),
    )(stored(keys), stored(values))


def split_queries_kernel(q_ref, cos_ref, sin_ref, out_ref, held, made, sems, out_sems):
    chunk = 4
    arrivals, leaves = [], []
    for part in range(GROUPS // chunk):
        here = pl.ds(part * chunk, chunk)
        arrivals.append(pltpu.make_async_copy(q_ref.at[here], held.at[here], sems.at[part]))
        leaves.append(
            pltpu.make_async_copy(made.at[:, here], out_ref.at[:, here], out_sems.at[part])
        )
    for copy in arrivals:
        copy.start()
    for part in range(GROUPS // chunk):
        arrivals[part].wait()

        def one_group(index, _):
            group = part * chunk + index
            cosine, sine = cos_ref[group], sin_ref[group]
            for head in range(QUERY_HEADS):
                turned = rotated(held[group, :, pl.ds(head * WIDTH, WIDTH)], cosine, sine)
                made[head // PER_KV, group, head % PER_KV] = turned.astype(jnp.bfloat16)
            return 0

        lax.fori_loop(0, chunk, one_group, 0)
        leaves[part].start()
    for copy in leaves:
        copy.wait()


def split_queries(queries, cosine, sine):
    shape = (KEY_VALUE_HEADS, GROUPS, PER_KV, ROWS, WIDTH)
    return pl.pallas_call(
        split_queries_kernel,
        in_specs=[HBM, VMEM, VMEM],
        out_specs=HBM,
        out_shape=pltpu.HBM(shape, jnp.bfloat16),
        scratch_shapes=[
            pltpu.VMEM((GROUPS, ROWS, QUERY_HEADS * WIDTH), jnp.bfloat16),
            pltpu.VMEM(shape, jnp.bfloat16),
            pltpu.SemaphoreType.DMA((4,)),
            pltpu.SemaphoreType.DMA((4,)),
        ],
        cost_estimate=pl.CostEstimate(
            flops=10_000_000, bytes_accessed=6_500_000, transcendentals=0
        ),
        **small(16, name="split_queries"),
    )(stored(queries), resident(cosine), resident(sine))


def join_heads_kernel(in_ref, out_ref, held, sems):
    chunk = 4
    copies = []
    for part in range(GROUPS // chunk):

        def one_group(index, _):
            group = part * chunk + index
            for head in range(QUERY_HEADS):
                held[group, :, pl.ds(head * WIDTH, WIDTH)] = in_ref[
                    head // PER_KV, group, head % PER_KV
                ]
            return 0

        lax.fori_loop(0, chunk, one_group, 0)
        here = pl.ds(part * chunk, chunk)
        copies.append(pltpu.make_async_copy(held.at[here], out_ref.at[here], sems.at[part]))
        copies[-1].start()
    for copy in copies:
        copy.wait()


def join_heads(parts):
    return pl.pallas_call(
        join_heads_kernel,
        in_specs=[VMEM],
        out_specs=HBM,
        out_shape=pltpu.HBM((GROUPS, ROWS, QUERY_HEADS * WIDTH), jnp.bfloat16),
        scratch_shapes=[
            pltpu.VMEM((GROUPS, ROWS, QUERY_HEADS * WIDTH), jnp.bfloat16),
            pltpu.SemaphoreType.DMA((4,)),
        ],
        **small(16, name="join_heads"),
    )(resident(parts))


def turn_keys_kernel(in_ref, cos_ref, sin_ref, *out_refs):
    for slot in range(SLOTS):
        own_ref, far_ref = out_refs[slot], out_refs[SLOTS + slot]
        keys = in_ref[:, slot, 0].astype(jnp.float32).reshape(PAIR, WIDTH)
        values = in_ref[:, slot, 1].astype(jnp.float32).reshape(PAIR, WIDTH)
        keys = rotated(keys, cos_ref[slot], sin_ref[slot]).astype(jnp.bfloat16)
        values = values.astype(jnp.bfloat16)
        own_ref[:, :WIDTH] = keys
        own_ref[:, WIDTH:] = values
        far_ref[:, :WIDTH] = keys[PAIR - FAR :]
        far_ref[:, WIDTH:] = values[PAIR - FAR :]


def turn_keys(own, cosine, sine):
    return pl.pallas_call(
        turn_keys_kernel,
        in_specs=[VMEM] * 3,
        out_specs=[VMEM] * 4,
        out_shape=[jax.ShapeDtypeStruct((PAIR, 2 * WIDTH), jnp.bfloat16)] * 2
        + [jax.ShapeDtypeStruct((FAR, 2 * WIDTH), jnp.bfloat16)] * 2,
        **small(12, name="turn_keys"),
    )(own, cosine, sine)


def attend_kernel(
    order_ref, most_ref, base_ref, flag_ref, ends_ref, q_ref, own0, own1, near0, near1, far0, far1,
    out_ref, q_held, k_ref, v_ref, start_ref, bias_ref, s_ref, p_ref, q_sems, k_sems, v_sems,
):
    pieces = []
    for place, (pair, base, flag) in enumerate((
        ((own0, own1), PAD + HALO, 0),
        ((near0, near1), PAD + FAR, flag_ref[1]),
        ((far0, far1), PAD, flag_ref[0]),
    )):
        for index, ref in enumerate(pair):
            to = (flag + index) % SLOTS
            rows = pl.ds(base, ref.shape[0])
            for column, (held, sems) in enumerate(((k_ref, k_sems), (v_ref, v_sems))):
                pieces.append(
                    pltpu.make_async_copy(
                        ref.at[:, pl.ds(column * WIDTH, WIDTH)],
                        held.at[to, rows, :],
                        sems.at[place * SLOTS + index],
                    )
                )
    for copy in pieces:
        copy.start()

    def arrival(index):
        slot, step = index // STEPS, index % STEPS
        return pltpu.make_async_copy(
            q_ref.at[pl.ds(step * SOURCES, SOURCES), slot], q_held.at[index], q_sems.at[index]
        )

    for index in range(UNITS):
        arrival(order_ref[index]).start()
    for slot in range(SLOTS):
        k_ref[slot, :PAD, :] = jnp.zeros((PAD, WIDTH), jnp.bfloat16)
        v_ref[slot, :PAD, :] = jnp.zeros((PAD, WIDTH), jnp.bfloat16)
    for index in range(UNITS):
        base = base_ref[index // STEPS]
        ends = jnp.broadcast_to(ends_ref[...] - base, (TILE, WIDTH))
        own = PAD + HALO + index % STEPS * TILE
        own = own + lax.broadcasted_iota(jnp.int32, (TILE, WIDTH), 0)
        start = jnp.max(jnp.where(ends <= own, ends, -base), axis=1, keepdims=True)
        start_ref[index] = jnp.broadcast_to(start, (TILE, WIDTH))
    for copy in pieces:
        copy.wait()

    def one_team(team, _):
        units = [order_ref[team * TEAM + i] for i in range(TEAM)]
        slots = [unit // STEPS for unit in units]
        steps = [unit % STEPS for unit in units]
        stops = [step * TILE + REACH for step in steps]
        for unit in units:
            arrival(unit).wait()

        for count in range(1, MOST + 1):

            @pl.when(most_ref[team] == count)
            def _():
                width = count * WINDOW
                begins = [pl.multiple_of(stop - width, 16) for stop in stops]

                def score(i):
                    lane = lax.broadcasted_iota(jnp.int32, (TILE, WIDTH), 1) + begins[i]
                    row = stops[i] - TILE + lax.broadcasted_iota(jnp.int32, (TILE, WIDTH), 0)
                    start = start_ref[units[i]]
                    for column in range(0, width, WIDTH):
                        key = lane + column
                        allowed = (key >= start) & (key <= row)
                        bias_ref[i, :, pl.ds(column, WIDTH)] = jnp.where(allowed, 0.0, LOW)
                    q = q_held[units[i]].reshape(SIZE, WIDTH)
                    top = None
                    for window in range(count):
                        here = pl.ds(pl.multiple_of(begins[i] + window * WINDOW, 16), WINDOW)
                        scores = lax.dot_general(
                            q,
                            k_ref[slots[i], here, :],
                            (((1,), (1,)), ((), ())),
                            preferred_element_type=jnp.float32,
                        )
                        bias = bias_ref[i, :, pl.ds(window * WINDOW, WINDOW)]
                        scores = scores.reshape(SOURCES, PER_KV, ROWS, WINDOW)
                        scores = scores + bias.reshape(SOURCES, 1, ROWS, WINDOW)
                        scores = scores.reshape(SIZE, WINDOW)
                        s_ref[i, :, pl.ds(window * WINDOW, WINDOW)] = scores
                        high = jnp.maximum(scores[:, :WIDTH], scores[:, WIDTH:])
                        top = high if top is None else jnp.maximum(top, high)
                    top = jnp.max(top.astype(jnp.bfloat16), axis=1, keepdims=True)
                    return top.astype(jnp.float32)

                def weigh(i, top):
                    total = None
                    for window in range(count):
                        here = pl.ds(window * WINDOW, WINDOW)
                        weights = jnp.exp2((s_ref[i, :, here] - top) * SCALE)
                        p_ref[i, :, here] = weights.astype(jnp.bfloat16)
                        both = weights[:, :WIDTH] + weights[:, WIDTH:]
                        total = both if total is None else total + both
                    return jnp.sum(total, axis=1, keepdims=True)

                def mix(i, total):
                    mixed = jnp.dot(
                        p_ref[i, :, :width],
                        v_ref[slots[i], pl.ds(begins[i], width), :],
                        preferred_element_type=jnp.float32,
                    )
                    result = (mixed / total).astype(jnp.bfloat16)
                    out_ref[pl.ds(steps[i] * SOURCES, SOURCES), slots[i]] = result.reshape(
                        SOURCES, PIECE, WIDTH
                    )

                tops = [score(0)]
                for i in range(TEAM):
                    if i + 1 < TEAM:
                        tops.append(score(i + 1))
                    mix(i, weigh(i, tops[i]))

        return 0

    lax.fori_loop(0, UNITS // TEAM, one_team, 0)


def attend(order, most, base, flags, ends, q, own, near, far):
    return pl.pallas_call(
        attend_kernel,
        in_specs=[SMEM] * 4 + [VMEM] + [HBM] * 7,
        out_specs=VMEM,
        out_shape=pltpu.VMEM((PEERS, SLOTS, PIECE, WIDTH), jnp.bfloat16),
        scratch_shapes=[
            pltpu.VMEM((UNITS, SOURCES, PIECE, WIDTH), jnp.bfloat16),
            pltpu.VMEM((SLOTS, KEYS, WIDTH), jnp.bfloat16),
            pltpu.VMEM((SLOTS, KEYS, WIDTH), jnp.bfloat16),
            pltpu.VMEM((UNITS, TILE, WIDTH), jnp.int32),
            pltpu.VMEM((TEAM, TILE, REACH), jnp.float32),
            pltpu.VMEM((TEAM, SIZE, REACH), jnp.float32),
            pltpu.VMEM((TEAM, SIZE, REACH), jnp.bfloat16),
            pltpu.SemaphoreType.DMA((UNITS,)),
            pltpu.SemaphoreType.DMA((3 * SLOTS,)),
            pltpu.SemaphoreType.DMA((3 * SLOTS,)),
        ],
        cost_estimate=pl.CostEstimate(
            flops=8_000_000_000, bytes_accessed=10_000_000, transcendentals=12_000_000
        ),
        **small(32, name="attend"),
    )(order, most, base, flags, ends, *map(stored, (q,) + own + near + far))


def exchange(value):
    return lax.all_to_all(value, ("zh", "dp"), split_axis=0, concat_axis=0, tiled=True)


def moved(value, slot, steps):
    pairs = []
    for dp in range(16):
        for x in range(4):
            to = dp
            if x + steps >= 4 and slot == 1:
                if dp % 8 == 7:
                    continue
                to = dp + 1
            for h in range(2):
                pairs.append((dp * 8 + x * 2 + h, to * 8 + (x + steps) % 4 * 2 + h))
    return lax.ppermute(value, ("dp", "x", "zh"), pairs)


def tables(positions):
    lane = jnp.arange(WIDTH, dtype=jnp.int32)
    exponent = (lane % HALF).astype(jnp.float32) * (2.0 / WIDTH)
    frequency = jnp.exp(-exponent * jnp.log(jnp.float32(ROPE_THETA)))
    angles = positions.astype(jnp.float32)[..., None] * frequency
    return jnp.cos(angles), jnp.sin(angles) * jnp.where(lane < HALF, -1.0, 1.0)


def on_device(queries, keys, values, doc_lengths):
    dp, x, zh = lax.axis_index("dp"), lax.axis_index("x"), lax.axis_index("zh")
    own = split_keys(keys.reshape(GROUPS, ROWS, -1), values.reshape(GROUPS, ROWS, -1))
    own = exchange(own.reshape(PEERS, SLOTS, 2, ROWS, WIDTH))

    home = (
        jnp.arange(GROUPS, dtype=jnp.int32)[:, None] * GROUP
        + (x * 2 + zh) * (PAIR // 2)
        + dp * ROWS
        + jnp.arange(ROWS, dtype=jnp.int32)[None, :]
    )
    base = (dp % 8 * SLOTS + jnp.arange(SLOTS, dtype=jnp.int32)) * GROUP + x * PAIR
    positions = base[:, None] + jnp.arange(PAIR, dtype=jnp.int32)[None, :]
    turns = lax.optimization_barrier((*tables(home), *tables(positions)))
    q = split_queries(queries.reshape(GROUPS, ROWS, -1), *turns[:2])
    q = exchange(q.reshape(PEERS, SLOTS, PER_KV, ROWS, WIDTH))

    own0, own1, last0, last1 = turn_keys(own, *turns[2:])
    near = moved(own0, 0, 1), moved(own1, 1, 1)
    far = moved(last0, 0, 2), moved(last1, 1, 2)
    flags = jnp.stack([(x < 2).astype(jnp.int32), (x < 1).astype(jnp.int32)])

    docs = jnp.arange(WIDTH, dtype=jnp.int32)
    lengths = jnp.pad(doc_lengths, (0, WIDTH - doc_lengths.shape[0]))
    ends = jnp.sum(jnp.where(docs[:, None] <= docs[None, :], lengths[:, None], 0), axis=0)
    heads = base[:, None] + jnp.arange(0, PAIR, TILE, dtype=jnp.int32)[None, :]
    first = jnp.max(jnp.where(ends <= heads[..., None], ends, 0), axis=-1)
    need = (heads + TILE - first + WINDOW - 1) // WINDOW
    need, unit = need.reshape(-1), jnp.arange(UNITS, dtype=jnp.int32)
    earlier = (need[None, :] > need[:, None]) | (
        (need[None, :] == need[:, None]) & (unit[None, :] < unit[:, None])
    )
    rank = jnp.sum(earlier.astype(jnp.int32), axis=1)
    order = jnp.sum(jnp.where(rank[None, :] == unit[:, None], unit[None, :], 0), axis=1)
    most = jnp.sum(jnp.where(rank[None, :] == unit[::TEAM, None], need[None, :], 0), axis=1)
    base = base - PAD - HALO

    mixed = attend(
        order,
        most,
        base,
        flags,
        ends[None, :],
        q.reshape(PEERS, SLOTS, PIECE, WIDTH),
        (own0, own1),
        near,
        far,
    )
    back = exchange(mixed.reshape(PEERS, SLOTS, PER_KV, ROWS, WIDTH))
    back = join_heads(back.reshape(KEY_VALUE_HEADS, GROUPS, PER_KV, ROWS, WIDTH))
    return back.reshape(queries.shape)


def solution(mesh):
    fine = Mesh(mesh.devices.reshape(16, 4, 2), ("dp", "x", "zh"))
    spec = P(None, ("x", "zh"), "dp", None)
    return jax.shard_map(
        on_device, mesh=fine, in_specs=(spec, spec, spec, P()), out_specs=spec, check_vma=False
    )
```
